32 devices in a mesh: groups: 2 (over y), grid: 4 (over x, core), mesh: 4 (over z).
Axes of the slice: x: 2, y: 2, z: 4, core: 2. Of those that a mesh axis runs over, the one named last changes fastest.
Arguments:
- grid_in: bfloat16 [227, 16384], P(None, ('groups', 'grid', 'mesh')), parts along dimension 1, may hold values from -6 to 6
- grid_cot: bfloat16 [227, 16384], P(None, ('groups', 'grid', 'mesh')), parts along dimension 1, may hold values from -0.15625 to 0.15625
- enc_src: int32 [256, 4], P(('grid', 'mesh')), may hold values from 0 to 511
- enc_feat: bfloat16 [4, 1024], P(None, ('grid', 'mesh')), may hold values from -6 to 6
- enc_dst: int32 [256, 4], P(('grid', 'mesh')), may hold values from 0 to 63
- enc_count: int32 [256], P(('grid', 'mesh')), may hold values from 1 to 4, as said below
- halo_up: int32 [512], P('mesh'), may hold values from 0 to 255
- halo_down: int32 [512], P('mesh'), may hold values from 0 to 255
- proc_src: int32 [32768], P(('grid', 'mesh')), may hold values from 0 to 511
- proc_dst: int32 [32768], P(('grid', 'mesh')), may hold values from 0 to 63
- dec_send: int32 [256, 4], P(('grid', 'mesh')), may hold values from 0 to 63
- dec_row: int32 [256, 4], P(('grid', 'mesh')), may hold values from 0 to 511
- dec_count: int32 [256], P(('grid', 'mesh')), may hold values from 1 to 4, as said below
- embed_first: bfloat16 [227, 512], replicated, may hold values from -0.375 to 0.375
- embed_second: bfloat16 [512, 512], replicated, may hold values from -0.25 to 0.25
- edge_weight: bfloat16 [512, 512], replicated, may hold values from -0.25 to 0.25
- feature_weight: bfloat16 [4, 512], replicated, may hold values from -3 to 3
- layer_edge_in: bfloat16 [1, 1024, 512], replicated, may hold values from -0.1875 to 0.1875
- layer_edge_out: bfloat16 [1, 512, 512], replicated, may hold values from -0.25 to 0.25
- layer_node_in: bfloat16 [1, 1024, 512], replicated, may hold values from -0.1875 to 0.1875
- layer_node_out: bfloat16 [1, 512, 512], replicated, may hold values from -0.25 to 0.25
- out_first: bfloat16 [1024, 512], replicated, may hold values from -0.1875 to 0.1875
- out_second: bfloat16 [227, 512], replicated, may hold values from -0.25 to 0.25
Outputs:
- delta: bfloat16 [227, 16384], P(None, ('groups', 'grid', 'mesh')), parts along dimension 1
- grad_embed_first: float32 [454, 512], P('groups', ('grid', 'mesh')), parts along dimension 0
- grad_embed_second: float32 [1024, 512], P('groups', ('grid', 'mesh')), parts along dimension 0
- grad_edge: float32 [1024, 512], P('groups', ('grid', 'mesh')), parts along dimension 0
- grad_feature: float32 [8, 512], P('groups', ('grid', 'mesh')), parts along dimension 0
- grad_edge_in: float32 [2, 1024, 512], P('groups', None, ('grid', 'mesh')), parts along dimension 0
- grad_edge_out: float32 [2, 512, 512], P('groups', None, ('grid', 'mesh')), parts along dimension 0
- grad_node_in: float32 [2, 1024, 512], P('groups', None, ('grid', 'mesh')), parts along dimension 0
- grad_node_out: float32 [2, 512, 512], P('groups', None, ('grid', 'mesh')), parts along dimension 0
- grad_out_first: float32 [2048, 512], P('groups', ('grid', 'mesh')), parts along dimension 0
- grad_out_second: float32 [454, 512], P('groups', ('grid', 'mesh')), parts along dimension 0
The draws below stay inside these ranges and needn't reach their ends.
There are 2 independent parts, one for each index of `groups`. The reference program is written for one: setup_inputs(seed, part) draws one part's arguments, and reference() takes and returns one part's arrays. A program takes and returns all parts, laid end to end along the dimension named above; an argument that names none is the same for every part. Nothing has to cross between parts.
Inputs may be any that keep to these rules, and one draw needn't show every extreme that they name: `enc_count`: live encoder slots of each block; one owner has 4 live slots from every tile. `dec_count`: live decoder slots of each block; one tile has 4 live slots from every owner.
All inputs are finite; a program needn't handle non-finite values.
Results may differ from the reference program's by a relative error of at most 0.025.
Values may be sent and summed in bfloat16 or wider, within the bound.
A program may use at most 128 MiB of HBM per device.

```python
import jax
import jax.numpy as jnp
from jax import lax

C = 227
W = 512
EF = 4
LAYERS = 1
CAP = 4
DCAP = 4
G_DEV = 512
MESH_DEV = 64
E_DEV = 2048
HALO = 128
TILES = 16
PART = 256
GRID = 8192
N_GRID = 4
N_MESH = 4


def full_counts(key, most):
    key_counts, key_full = jax.random.split(key)
    counts = jax.random.randint(key_counts, (TILES, TILES), 1, most + 1)
    chosen = jax.random.randint(key_full, (), 0, TILES)
    is_full = jnp.arange(TILES, dtype=jnp.int32)[:, None] == chosen
    return jnp.where(is_full, most, counts).reshape(-1).astype(jnp.int32)


def draw_enc_count(key, part):
    key = jax.random.fold_in(key, 11)
    return full_counts(key, CAP)


def draw_dec_count(key, part):
    key = jax.random.fold_in(key, 12)
    return full_counts(key, DCAP)


def with_ends(values, own_key, smallest, high):
    shape = values.shape
    spot = [jax.random.randint(jax.random.fold_in(own_key, axis), (), 0, shape[axis]) for axis in range(len(shape))]
    values = values.at[tuple(spot)].set(smallest)
    longest = shape.index(max(shape))
    spot[longest] = (spot[longest] + 1) % shape[longest]
    return values.at[tuple(spot)].set(high)


def block_levels(stream_key, dims, pieces, smallest, top_value):
    level = 1.0
    for dim, parts in pieces:
        draws = jax.random.uniform(jax.random.fold_in(jax.random.fold_in(stream_key, 6), dim), (parts,), jnp.float32, smallest / len(pieces), top_value / len(pieces))
        level = level * jnp.repeat(jnp.exp(draws), dims[dim] // parts).reshape((-1,) + (1,) * (len(dims) - 1 - dim))
    return level


def scatter_about(key, dims, spread, bound, shards=(), kind=jnp.bfloat16):
    loudness = block_levels(key, dims, shards, -0.22, 0.18) if shards else 1.0
    array = jax.random.normal(key, dims, jnp.float32) * spread * loudness
    return jnp.minimum(jnp.maximum(array, -bound), bound).astype(kind)


def setup_inputs(seed: int = 0, part: int = 0) -> dict:
    key_of = jax.random.split(jax.random.key(seed), 24)
    own_keys = jax.random.split(jax.random.fold_in(key_of[23], part), 24)
    grid_in = scatter_about(own_keys[0], (C, GRID), 1.0, 6.0, ((1, 16),))
    grid_cot = scatter_about(own_keys[1], (C, GRID), ((G_DEV * TILES) ** -0.5), 0.15625, ((1, 16),))
    enc_src = with_ends(jax.random.randint(key_of[2], (TILES * TILES, CAP), 0, G_DEV), jax.random.fold_in(key_of[2], 1), 0, G_DEV - 1).astype(jnp.int32)
    enc_feat = scatter_about(key_of[3], (EF, TILES * TILES * CAP), 1.0, 6.0, ((1, 16),))
    enc_dst = with_ends(jax.random.randint(key_of[4], (TILES * TILES, CAP), 0, MESH_DEV), jax.random.fold_in(key_of[4], 1), 0, MESH_DEV - 1).astype(jnp.int32)
    enc_count = draw_enc_count(jax.random.fold_in(key_of[23], 71), part)
    halo_up = with_ends(jax.random.randint(key_of[6], (N_MESH * HALO,), 0, PART), jax.random.fold_in(key_of[6], 1), 0, PART - 1).astype(jnp.int32)
    halo_down = with_ends(jax.random.randint(key_of[7], (N_MESH * HALO,), 0, PART), jax.random.fold_in(key_of[7], 1), 0, PART - 1).astype(jnp.int32)
    proc_src = with_ends(jax.random.randint(key_of[8], (TILES * E_DEV,), 0, PART + 2 * HALO), jax.random.fold_in(key_of[8], 1), 0, (PART + 2 * HALO) - 1).astype(jnp.int32)
    proc_dst = with_ends(jax.random.randint(key_of[9], (TILES * E_DEV,), 0, MESH_DEV), jax.random.fold_in(key_of[9], 1), 0, MESH_DEV - 1).astype(jnp.int32)
    dec_send = with_ends(jax.random.randint(key_of[10], (TILES * TILES, DCAP), 0, MESH_DEV), jax.random.fold_in(key_of[10], 1), 0, MESH_DEV - 1).astype(jnp.int32)
    dec_row = with_ends(jax.random.randint(key_of[11], (TILES * TILES, DCAP), 0, G_DEV), jax.random.fold_in(key_of[11], 1), 0, G_DEV - 1).astype(jnp.int32)
    dec_count = draw_dec_count(jax.random.fold_in(key_of[23], 71), part)
    embed_first = scatter_about(key_of[13], (C, W), C ** -0.5, 0.375)
    embed_second = scatter_about(key_of[14], (W, W), W ** -0.5, 0.25)
    edge_weight = scatter_about(key_of[15], (W, W), W ** -0.5, 0.25)
    feature_weight = scatter_about(key_of[16], (EF, W), EF ** -0.5, 3.0)
    layer_edge_in = scatter_about(key_of[17], (LAYERS, 2 * W, W), (2 * W) ** -0.5, 0.1875)
    layer_edge_out = scatter_about(key_of[18], (LAYERS, W, W), W ** -0.5, 0.25)
    layer_node_in = scatter_about(key_of[19], (LAYERS, 2 * W, W), (2 * W) ** -0.5, 0.1875)
    layer_node_out = scatter_about(key_of[20], (LAYERS, W, W), W ** -0.5, 0.25)
    out_first = scatter_about(key_of[21], (2 * W, W), (2 * W) ** -0.5, 0.1875)
    out_second = scatter_about(key_of[22], (C, W), W ** -0.5, 0.25)
    return dict(grid_in=grid_in, grid_cot=grid_cot, enc_src=enc_src, enc_feat=enc_feat, enc_dst=enc_dst, enc_count=enc_count, halo_up=halo_up, halo_down=halo_down, proc_src=proc_src, proc_dst=proc_dst, dec_send=dec_send, dec_row=dec_row, dec_count=dec_count, embed_first=embed_first, embed_second=embed_second, edge_weight=edge_weight, feature_weight=feature_weight, layer_edge_in=layer_edge_in, layer_edge_out=layer_edge_out, layer_node_in=layer_node_in, layer_node_out=layer_node_out, out_first=out_first, out_second=out_second)


def round_low(values):
    return lax.optimization_barrier(values.astype(jnp.bfloat16)).astype(jnp.float32)

def plain_product(left, right):
    return jnp.dot(left.astype(jnp.bfloat16), right.astype(jnp.bfloat16), preferred_element_type=jnp.float32)

def product_forward(left, right):
    return (plain_product(left, right), (left, right))

def product_backward(saved, incoming):
    left, right = saved
    grad_low = incoming.astype(jnp.bfloat16)
    grad_left = jnp.dot(grad_low, right.astype(jnp.bfloat16).T, preferred_element_type=jnp.float32)
    grad_right = jnp.dot(left.astype(jnp.bfloat16).T, grad_low, preferred_element_type=jnp.float32)
    return (grad_left, grad_right)

def product(left, right):
    core = jax.custom_vjp(plain_product)
    core.defvjp(product_forward, product_backward)
    return core(left, right)

def one_hot(targets, count):
    return (targets[None, :] == jnp.arange(count, dtype=jnp.int32)[:, None]).astype(jnp.float32)

def embed_grid(grid_tile, first, second):
    hidden = round_low(jax.nn.silu(product(grid_tile.astype(jnp.float32).T, first)))
    return round_low(product(hidden, second))

def send_messages(grid_latent, senders, features, edge_weight, feature_weight):
    rows = jnp.take(grid_latent, senders, axis=0)
    summed = product(rows, edge_weight) + product(features.astype(jnp.float32).T, feature_weight)
    return round_low(jax.nn.silu(summed))

def gather_mesh(received, targets, count):
    total = product(one_hot(targets, count), received)
    scale = lax.rsqrt(lax.optimization_barrier(jnp.mean(total * total, axis=-1, keepdims=True)) + 1e-05)
    return round_low(total * scale)

def process_layer(latent, extended, senders, targets, edge_in, edge_out, node_in, node_out):
    pairs = jnp.concatenate([jnp.take(extended, senders, axis=0), jnp.take(latent, targets, axis=0)], axis=1)
    hidden = round_low(jax.nn.silu(product(pairs, edge_in)))
    messages = round_low(product(hidden, edge_out))
    summed = round_low(product(one_hot(targets, latent.shape[0]), messages))
    joined = jnp.concatenate([latent, summed], axis=1)
    inner = round_low(jax.nn.silu(product(joined, node_in)))
    return round_low(latent + product(inner, node_out))

def collect_grid(received, targets, count):
    return round_low(product(one_hot(targets, count), received))

def decode_grid(grid_latent, collected, out_first, out_second):
    joined = jnp.concatenate([grid_latent, collected], axis=1)
    inner = round_low(jax.nn.silu(product(joined, out_first)))
    return product(inner, out_second.T).T

def take_rows(table, picks):
    return jnp.take(table, picks, axis=0)

def forward(weights, grid_in, enc_src, enc_feat, enc_dst, enc_count, halo_up, halo_down, proc_src, proc_dst, dec_send, dec_row, dec_count):
    embed_first, embed_second, edge_weight, feature_weight, edge_in, edge_out, node_in, node_out, out_first, out_second = weights
    tile_grid = grid_in.reshape(C, TILES, G_DEV).transpose(1, 0, 2)
    grid_latent = jax.vmap(lambda tile_rows: embed_grid(tile_rows, embed_first, embed_second))(tile_grid)
    senders = enc_src.reshape(TILES, TILES * CAP)
    features = enc_feat.reshape(EF, TILES, TILES * CAP).transpose(1, 0, 2)
    messages = jax.vmap(lambda latent_rows, send_rows, feature_rows: send_messages(latent_rows, send_rows, feature_rows, edge_weight, feature_weight))(grid_latent, senders, features)
    received = messages.reshape(TILES, TILES, CAP, W).transpose(1, 0, 2, 3).reshape(TILES, TILES * CAP, W)
    enc_valid = jnp.arange(CAP, dtype=jnp.int32)[None, None, :] < enc_count.reshape(TILES, TILES)[:, :, None]
    enc_targets = jnp.where(enc_valid, enc_dst.reshape(TILES, TILES, CAP), -1).reshape(TILES, TILES * CAP)
    latent = jax.vmap(lambda arrived, target_rows: gather_mesh(arrived, target_rows, MESH_DEV))(received, enc_targets)
    up_lists = halo_up.reshape(N_MESH, HALO)
    down_lists = halo_down.reshape(N_MESH, HALO)
    send_grid = proc_src.reshape(N_GRID, N_MESH, E_DEV)
    target_grid = proc_dst.reshape(N_GRID, N_MESH, E_DEV)
    for layer_index in range(LAYERS):
        table = latent.reshape(N_GRID, N_MESH, MESH_DEV, W).transpose(1, 0, 2, 3).reshape(N_MESH, PART, W)
        sent_up = jax.vmap(take_rows)(table, up_lists)
        sent_down = jax.vmap(take_rows)(table, down_lists)
        blank = jnp.zeros((1, HALO, W), jnp.float32)
        below = jnp.concatenate([blank, sent_up[:-1]], axis=0)
        above = jnp.concatenate([sent_down[1:], blank], axis=0)
        extended = jnp.concatenate([below, table, above], axis=1)
        weights_now = (edge_in[layer_index], edge_out[layer_index], node_in[layer_index], node_out[layer_index])

        def step_layer(latent_rows, extended_rows, send_rows, target_rows):
            return process_layer(latent_rows, extended_rows, send_rows, target_rows, *weights_now)
        inner_map = jax.vmap(step_layer, in_axes=(0, 0, 0, 0))
        outer_map = jax.vmap(inner_map, in_axes=(0, None, 0, 0))
        latent = outer_map(latent.reshape(N_GRID, N_MESH, MESH_DEV, W), extended, send_grid, target_grid).reshape(TILES, MESH_DEV, W)
    sent = jax.vmap(take_rows)(latent, dec_send.reshape(TILES, TILES * DCAP))
    arrived = sent.reshape(TILES, TILES, DCAP, W).transpose(1, 0, 2, 3).reshape(TILES, TILES * DCAP, W)
    dec_valid = jnp.arange(DCAP, dtype=jnp.int32)[None, None, :] < dec_count.reshape(TILES, TILES)[:, :, None]
    dec_targets = jnp.where(dec_valid, dec_row.reshape(TILES, TILES, DCAP), -1).reshape(TILES, TILES * DCAP)
    collected = jax.vmap(lambda arrived_rows, target_rows: collect_grid(arrived_rows, target_rows, G_DEV))(arrived, dec_targets)
    outputs = jax.vmap(lambda latent_rows, collected_rows: decode_grid(latent_rows, collected_rows, out_first, out_second))(grid_latent, collected)
    return outputs.transpose(1, 0, 2).reshape(C, TILES * G_DEV)

def reference(grid_in, grid_cot, enc_src, enc_feat, enc_dst, enc_count, halo_up, halo_down, proc_src, proc_dst, dec_send, dec_row, dec_count, embed_first, embed_second, edge_weight, feature_weight, layer_edge_in, layer_edge_out, layer_node_in, layer_node_out, out_first, out_second):
    weights = tuple((matrix.astype(jnp.float32) for matrix in (embed_first, embed_second, edge_weight, feature_weight, layer_edge_in, layer_edge_out, layer_node_in, layer_node_out, out_first, out_second)))

    def model(weight_set):
        return forward(weight_set, grid_in, enc_src, enc_feat, enc_dst, enc_count, halo_up, halo_down, proc_src, proc_dst, dec_send, dec_row, dec_count)
    delta_full, pullback = jax.vjp(model, weights)
    grads = pullback(grid_cot.astype(jnp.float32))[0]
    return (delta_full.astype(jnp.bfloat16), grads[0], grads[1], grads[2], grads[3], grads[4], grads[5], grads[6], grads[7], grads[8], grads[9])
```

```python
import jax
import jax.numpy as jnp
from jax import lax
from jax.sharding import PartitionSpec as P

G_DEV = 512
MESH_DEV = 64
LOW = jnp.bfloat16
TILE = ("grid", "mesh")


def mm(left, right, over_left=1, over_right=0):
    return lax.dot_general(
        left,
        right,
        (((over_left,), (over_right,)), ((), ())),
        preferred_element_type=jnp.float32,
    )


def low(values):
    return values.astype(LOW)


def wide(values):
    return values.astype(jnp.float32)


def hot(targets, count):
    return low(targets[:, None] == lax.broadcasted_iota(jnp.int32, (1, count), 1))


def hot_columns(targets, count):
    return low(targets[None, :] == lax.broadcasted_iota(jnp.int32, (count, 1), 0))


def silu_both(value):
    gate = 1.0 / (1.0 + jnp.exp(-value))
    return low(value * gate), gate * (1.0 + value * (1.0 - gate))


def route(values):
    return lax.all_to_all(values, TILE, split_axis=0, concat_axis=0, tiled=True)


def exchange(to_next, to_previous):
    count = lax.axis_size("mesh")
    forward = [(i, i + 1) for i in range(count - 1)]
    backward = [(i + 1, i) for i in range(count - 1)]
    from_previous = lax.ppermute(to_next, "mesh", forward)
    from_next = lax.ppermute(to_previous, "mesh", backward)
    return from_previous, from_next


def reduce_group(grads):
    padded = []
    for grad in grads:
        extra = -grad.shape[1] % 128
        padded.append(jnp.pad(low(grad), ((0, 0), (0, extra))) if extra else low(grad))
    whole = jnp.concatenate(padded, axis=1)
    part = lax.psum_scatter(whole, "grid", scatter_dimension=0, tiled=True)
    part = lax.psum_scatter(part, "mesh", scatter_dimension=0, tiled=True)
    part = wide(part)
    outs = []
    start = 0
    for grad, block in zip(grads, padded):
        outs.append(part[:, start : start + grad.shape[1]].T)
        start += block.shape[1]
    return outs


def on_device(
    grid_in,
    grid_cot,
    enc_src,
    enc_feat,
    enc_dst,
    enc_count,
    halo_up,
    halo_down,
    proc_src,
    proc_dst,
    dec_send,
    dec_row,
    dec_count,
    embed_first,
    embed_second,
    edge_weight,
    feature_weight,
    layer_edge_in,
    layer_edge_out,
    layer_node_in,
    layer_node_out,
    out_first,
    out_second,
):
    width = embed_second.shape[0]
    halo = halo_up.shape[0]
    capacity = enc_src.shape[1]
    dec_capacity = dec_send.shape[1]
    n_grid = lax.axis_size("grid")
    part = MESH_DEV * n_grid
    span = part + 2 * halo
    edge_in, edge_out = layer_edge_in[0], layer_edge_out[0]
    node_in, node_out = layer_node_in[0], layer_node_out[0]
    edge_in_send, edge_in_own = edge_in[:width], edge_in[width:]
    out_grid, out_mesh = out_first[:width], out_first[width:]

    pre_embed = mm(grid_in, embed_first, 0, 0)
    hid_embed, slope_embed = silu_both(pre_embed)
    grid_latent = low(mm(hid_embed, embed_second))

    send_hot = hot(enc_src.reshape(-1), G_DEV)
    rows = low(mm(send_hot, grid_latent))
    msg, slope_msg = silu_both(mm(rows, edge_weight) + mm(enc_feat, feature_weight, 0, 0))
    received = route(msg)

    enc_valid = jnp.arange(capacity, dtype=jnp.int32)[None, :] < enc_count[:, None]
    enc_hot = hot_columns(jnp.where(enc_valid, enc_dst, -1).reshape(-1), MESH_DEV)
    total = mm(enc_hot, received)
    scale = lax.rsqrt(jnp.mean(total * total, axis=-1, keepdims=True) + 1e-05)
    latent = low(total * scale)

    table = lax.all_gather(latent, "grid", axis=0, tiled=True)
    up_hot, down_hot = hot(halo_up, part), hot(halo_down, part)
    below, above = exchange(low(mm(up_hot, table)), low(mm(down_hot, table)))
    extended = jnp.concatenate([below, table, above], axis=0)

    mapped = low(
        jnp.concatenate([mm(extended, edge_in_send), mm(latent, edge_in_own)], axis=0)
    )
    places = lax.broadcasted_iota(jnp.int32, (1, span + MESH_DEV), 1)
    edge_hot = low(
        (proc_src[:, None] == places) | ((proc_dst + span)[:, None] == places)
    )
    own_hot = hot(proc_dst, MESH_DEV)
    hid_edge, slope_edge = silu_both(mm(edge_hot, mapped))
    hid_sum = low(mm(own_hot, hid_edge, 0, 0))
    edge_sum = low(mm(hid_sum, edge_out))
    joined = jnp.concatenate([latent, edge_sum], axis=1)
    hid_node, slope_node = silu_both(mm(joined, node_in))
    final = low(wide(latent) + mm(hid_node, node_out))

    pick_hot = hot(dec_send.reshape(-1), MESH_DEV)
    arrived = route(low(mm(pick_hot, final)))

    dec_valid = jnp.arange(dec_capacity, dtype=jnp.int32)[None, :] < dec_count[:, None]
    dec_hot = hot_columns(jnp.where(dec_valid, dec_row, -1).reshape(-1), G_DEV)
    pre_out = mm(grid_latent, out_grid) + mm(dec_hot, low(mm(arrived, out_mesh)))
    hid_out, slope_out = silu_both(pre_out)
    delta = low(mm(out_second, hid_out, 1, 1))

    g_out = low(wide(low(mm(grid_cot, out_second, 0, 0))) * slope_out)
    g_out_mesh = low(mm(dec_hot, g_out, 0, 0))
    g_sent = route(low(mm(g_out_mesh, out_mesh, 1, 1)))
    g_final = low(mm(pick_hot, g_sent, 0, 0))
    g_node = low(wide(low(mm(g_final, node_out, 1, 1))) * slope_node)
    g_joined = mm(g_node, node_in, 1, 1)
    g_own = wide(g_final) + g_joined[:, :width]
    g_sum = low(g_joined[:, width:])
    g_hid = low(mm(g_sum, edge_out, 1, 1))
    g_edge = low(mm(own_hot, g_hid) * slope_edge)
    g_mapped = low(mm(edge_hot, g_edge, 0, 0))
    g_send_map, g_own_map = g_mapped[:span], g_mapped[span:]
    g_extended = mm(g_send_map, edge_in_send, 1, 1)

    to_down, to_up = exchange(
        low(g_extended[halo + part :]), low(g_extended[:halo])
    )
    g_table = (
        g_extended[halo : halo + part]
        + mm(down_hot, to_down, 0, 0)
        + mm(up_hot, to_up, 0, 0)
    )
    shares = lax.all_to_all(low(g_table), "grid", split_axis=0, concat_axis=0, tiled=True)
    g_latent = (
        g_own
        + mm(g_own_map, edge_in_own, 1, 1)
        + jnp.sum(wide(shares).reshape(n_grid, MESH_DEV, width), axis=0)
    )
    g_latent = wide(low(g_latent))
    normal = total * scale
    g_total = low(
        scale * (g_latent - normal * jnp.mean(g_latent * normal, axis=-1, keepdims=True))
    )
    g_msg = route(low(mm(enc_hot, g_total, 0, 0)))

    early = reduce_group(
        (
            jnp.concatenate(
                [mm(g_send_map, extended, 0, 0), mm(g_own_map, latent, 0, 0)], axis=1
            ),
            mm(g_sum, hid_sum, 0, 0),
            mm(g_node, joined, 0, 0),
            mm(g_final, hid_node, 0, 0),
            jnp.concatenate(
                [mm(g_out, grid_latent, 0, 0), mm(g_out_mesh, arrived, 0, 0)], axis=1
            ),
            mm(hid_out, grid_cot, 0, 1),
        )
    )

    g_pre = low(wide(g_msg) * slope_msg)
    g_rows = low(mm(g_pre, edge_weight, 1, 1))
    g_grid = low(mm(g_out, out_grid, 1, 1) + mm(send_hot, g_rows, 0, 0))
    g_embed = low(wide(low(mm(g_grid, embed_second, 1, 1))) * slope_embed)
    late = reduce_group(
        (
            mm(g_embed, grid_in, 0, 1),
            mm(g_grid, hid_embed, 0, 0),
            mm(g_pre, rows, 0, 0),
            mm(g_pre, enc_feat, 0, 1),
        )
    )
    layer = [grad[None] for grad in early[:4]]
    return (delta,) + tuple(late) + tuple(layer) + tuple(early[4:])


def solution(mesh):
    return jax.shard_map(
        on_device,
        mesh=mesh,
        in_specs=(
            P(None, ("groups", "grid", "mesh")),
            P(None, ("groups", "grid", "mesh")),
            P(("grid", "mesh"), None),
            P(None, ("grid", "mesh")),
            P(("grid", "mesh"), None),
            P(("grid", "mesh")),
            P("mesh"),
            P("mesh"),
            P(("grid", "mesh")),
            P(("grid", "mesh")),
            P(("grid", "mesh"), None),
            P(("grid", "mesh"), None),
            P(("grid", "mesh")),
            P(),
            P(),
            P(),
            P(),
            P(),
            P(),
            P(),
            P(),
            P(),
            P(),
        ),
        out_specs=(
            P(None, ("groups", "grid", "mesh")),
            P("groups", ("grid", "mesh")),
            P("groups", ("grid", "mesh")),
            P("groups", ("grid", "mesh")),
            P("groups", ("grid", "mesh")),
            P("groups", None, ("grid", "mesh")),
            P("groups", None, ("grid", "mesh")),
            P("groups", None, ("grid", "mesh")),
            P("groups", None, ("grid", "mesh")),
            P("groups", ("grid", "mesh")),
            P("groups", ("grid", "mesh")),
        ),
        check_vma=False,
    )
```

```python
import functools

import jax
import jax.numpy as jnp
from jax import lax
from jax.experimental import pallas as pl
from jax.experimental.pallas import tpu as pltpu
from jax.sharding import PartitionSpec as P

G_DEV = 512
MESH_DEV = 64
LOW = jnp.bfloat16
TILE = ("grid", "mesh")


def mm(left, right, over_left=1, over_right=0):
    return lax.dot_general(
        left,
        right,
        (((over_left,), (over_right,)), ((), ())),
        preferred_element_type=jnp.float32,
    )


def low(values):
    return values.astype(LOW)


def wide(values):
    return values.astype(jnp.float32)


def hot(targets, count):
    return low(targets[:, None] == lax.broadcasted_iota(jnp.int32, (1, count), 1))


def hot_columns(targets, count):
    return low(targets[None, :] == lax.broadcasted_iota(jnp.int32, (count, 1), 0))


def silu_both(value):
    gate = 1.0 / (1.0 + jnp.exp(-value))
    return low(value * gate), gate * (1.0 + value * (1.0 - gate))


def route(values):
    return lax.all_to_all(values, TILE, split_axis=0, concat_axis=0, tiled=True)


def exchange(to_next, to_previous):
    count = lax.axis_size("mesh")
    forward = [(i, i + 1) for i in range(count - 1)]
    backward = [(i + 1, i) for i in range(count - 1)]
    from_previous = lax.ppermute(to_next, "mesh", forward)
    from_next = lax.ppermute(to_previous, "mesh", backward)
    return from_previous, from_next


def join_grads(grads):
    padded = []
    for grad in grads:
        extra = -grad.shape[1] % 128
        padded.append(jnp.pad(low(grad), ((0, 0), (0, extra))) if extra else low(grad))
    return jnp.concatenate(padded, axis=1)


def split_grads(part, sizes):
    part = wide(part)
    outs = []
    start = 0
    for size in sizes:
        outs.append(part[:, start : start + size].T)
        start += size + (-size % 128)
    return outs


def plan_of(counts, order):
    left = dict(counts)
    bit = {"grid": 1, "mesh": 1}
    plan = []
    for axis in order:
        plan.append((axis, bit[axis], left["grid"], left["mesh"]))
        left[axis] //= 2
        bit[axis] *= 2
    return plan


def pieces_of(step, mine, rows):
    axis, bit, grids, meshes = step
    own = (mine[axis] // bit) % 2
    other = 1 - own
    pieces = []
    if axis == "grid":
        size = meshes * rows
        for high in range(grids // 2):
            pieces.append(((2 * high + own) * size, (2 * high + other) * size, high * size, size))
    else:
        for block in range(grids):
            for high in range(meshes // 2):
                base = block * meshes + 2 * high
                target = (block * (meshes // 2) + high) * rows
                pieces.append(((base + own) * rows, (base + other) * rows, target, rows))
    return pieces


def halving_kernel(counts, rows, spans, plans, x_ref, out_ref, *scratch):
    depth = len(plans[0])
    sums = [scratch[c * depth : (c + 1) * depth - 1] for c in range(len(spans))]
    base = len(spans) * depth
    lands = [scratch[base + c * depth : base + (c + 1) * depth] for c in range(len(spans))]
    sends, arrivals = scratch[-2], scratch[-1]
    mine = {"grid": lax.axis_index("grid"), "mesh": lax.axis_index("mesh")}

    def partner(axis, bit):
        return mine[axis] + bit * (1 - 2 * ((mine[axis] // bit) % 2))

    partners = {(axis, bit) for axis, bit, _, _ in plans[0]}
    barrier = pltpu.get_barrier_semaphore()
    for axis, bit in sorted(partners):
        pl.semaphore_signal(
            barrier,
            inc=1,
            device_id={axis: partner(axis, bit)},
            device_id_type=pl.DeviceIdType.MESH,
        )
    pl.semaphore_wait(barrier, len(partners))

    started = []
    number = 0
    flying = {}

    def source(c, s):
        return (x_ref, spans[c][0]) if s == 0 else (sums[c][s - 1], 0)

    def start(c, s):
        nonlocal number
        axis, bit, _, _ = plans[c][s]
        ref, first = source(c, s)
        copies = []
        for _, away, target, size in pieces_of(plans[c][s], mine, rows):
            copy = pltpu.make_async_remote_copy(
                src_ref=ref.at[pl.ds(pl.multiple_of(away, 16), size), pl.ds(first, spans[c][1])],
                dst_ref=lands[c][s].at[pl.ds(target, size), :],
                send_sem=sends.at[number],
                recv_sem=arrivals.at[number],
                device_id={axis: partner(axis, bit)},
                device_id_type=pl.DeviceIdType.MESH,
            )
            number += 1
            copy.start()
            copies.append(copy)
            started.append(copy)
        flying[c, s] = copies

    def finish(c, s):
        ref, first = source(c, s)
        pieces = pieces_of(plans[c][s], mine, rows)
        for copy, (keep, _, target, size) in zip(flying[c, s], pieces):
            copy.wait_recv()
            value = ref[pl.ds(pl.multiple_of(keep, 16), size), pl.ds(first, spans[c][1])].astype(
                jnp.float32
            ) + lands[c][s][pl.ds(target, size), :].astype(jnp.float32)
            if s == depth - 1:
                out_ref[:, pl.ds(spans[c][0], spans[c][1])] = value
            else:
                sums[c][s][pl.ds(target, size), :] = value.astype(LOW)

    for c in range(len(spans)):
        start(c, 0)
    for s in range(depth):
        for c in range(len(spans)):
            finish(c, s)
            if s + 1 < depth:
                start(c, s + 1)
    for copy in started:
        copy.wait_send()


def halving_scatter(whole):
    counts = {"grid": lax.axis_size("grid"), "mesh": lax.axis_size("mesh")}
    tiles = counts["grid"] * counts["mesh"]
    rows = whole.shape[0] // tiles
    if rows % 16 or counts["grid"] & (counts["grid"] - 1) or counts["mesh"] & (counts["mesh"] - 1):
        return lax.psum_scatter(whole, TILE, scatter_dimension=0, tiled=True)
    columns = whole.shape[1]
    grid_steps = ["grid"] * (counts["grid"].bit_length() - 1)
    mesh_steps = ["mesh"] * (counts["mesh"].bit_length() - 1)
    cut = (columns * 6 // 10) // 128 * 128
    spans = ((0, cut), (cut, columns - cut))
    orders = (grid_steps + mesh_steps, grid_steps[:1] + mesh_steps + grid_steps[1:])
    plans = [plan_of(counts, order) for order in orders]
    depth = len(plans[0])
    heights = [whole.shape[0] >> (s + 1) for s in range(depth)]
    sums = []
    lands = []
    for _, size in spans:
        sums += [pltpu.VMEM((heights[s], size), LOW) for s in range(depth)]
        lands += [pltpu.VMEM((heights[s], size), LOW) for s in range(depth)]
    fake = {"grid": 0, "mesh": 0}
    total = sum(len(pieces_of(step, fake, rows)) for plan in plans for step in plan)
    return pl.pallas_call(
        functools.partial(halving_kernel, counts, rows, spans, plans),
        out_shape=jax.ShapeDtypeStruct((rows, columns), jnp.float32),
        in_specs=[pl.BlockSpec(memory_space=pltpu.VMEM)],
        out_specs=pl.BlockSpec(memory_space=pltpu.VMEM),
        scratch_shapes=sums
        + lands
        + [pltpu.SemaphoreType.DMA((total,)), pltpu.SemaphoreType.DMA((total,))],
        compiler_params=pltpu.CompilerParams(
            collective_id=1, has_side_effects=True, vmem_limit_bytes=24 * 2**20
        ),
        cost_estimate=pl.CostEstimate(flops=0, bytes_accessed=90 * 10**6, transcendentals=0),
    )(whole)


def on_device(
    grid_in,
    grid_cot,
    enc_src,
    enc_feat,
    enc_dst,
    enc_count,
    halo_up,
    halo_down,
    proc_src,
    proc_dst,
    dec_send,
    dec_row,
    dec_count,
    embed_first,
    embed_second,
    edge_weight,
    feature_weight,
    layer_edge_in,
    layer_edge_out,
    layer_node_in,
    layer_node_out,
    out_first,
    out_second,
):
    width = embed_second.shape[0]
    halo = halo_up.shape[0]
    capacity = enc_src.shape[1]
    dec_capacity = dec_send.shape[1]
    n_grid = lax.axis_size("grid")
    part = MESH_DEV * n_grid
    span = part + 2 * halo
    edge_in, edge_out = layer_edge_in[0], layer_edge_out[0]
    node_in, node_out = layer_node_in[0], layer_node_out[0]
    edge_in_send, edge_in_own = edge_in[:width], edge_in[width:]
    out_grid, out_mesh = out_first[:width], out_first[width:]

    pre_embed = mm(grid_in, embed_first, 0, 0)
    hid_embed, slope_embed = silu_both(pre_embed)
    grid_latent = low(mm(hid_embed, embed_second))

    send_hot = hot(enc_src.reshape(-1), G_DEV)
    rows = low(mm(send_hot, grid_latent))
    msg, slope_msg = silu_both(mm(rows, edge_weight) + mm(enc_feat, feature_weight, 0, 0))
    received = route(msg)

    enc_valid = jnp.arange(capacity, dtype=jnp.int32)[None, :] < enc_count[:, None]
    enc_hot = hot_columns(jnp.where(enc_valid, enc_dst, -1).reshape(-1), MESH_DEV)
    total = mm(enc_hot, received)
    scale = lax.rsqrt(jnp.mean(total * total, axis=-1, keepdims=True) + 1e-05)
    latent = low(total * scale)

    table = lax.all_gather(latent, "grid", axis=0, tiled=True)
    up_hot, down_hot = hot(halo_up, part), hot(halo_down, part)
    below, above = exchange(low(mm(up_hot, table)), low(mm(down_hot, table)))
    extended = jnp.concatenate([below, table, above], axis=0)

    mapped = low(
        jnp.concatenate([mm(extended, edge_in_send), mm(latent, edge_in_own)], axis=0)
    )
    places = lax.broadcasted_iota(jnp.int32, (1, span + MESH_DEV), 1)
    edge_hot = low(
        (proc_src[:, None] == places) | ((proc_dst + span)[:, None] == places)
    )
    own_hot = hot(proc_dst, MESH_DEV)
    hid_edge, slope_edge = silu_both(mm(edge_hot, mapped))
    hid_sum = low(mm(own_hot, hid_edge, 0, 0))
    edge_sum = low(mm(hid_sum, edge_out))
    joined = jnp.concatenate([latent, edge_sum], axis=1)
    hid_node, slope_node = silu_both(mm(joined, node_in))
    final = low(wide(latent) + mm(hid_node, node_out))

    pick_hot = hot(dec_send.reshape(-1), MESH_DEV)
    arrived = route(low(mm(pick_hot, final)))

    dec_valid = jnp.arange(dec_capacity, dtype=jnp.int32)[None, :] < dec_count[:, None]
    dec_hot = hot_columns(jnp.where(dec_valid, dec_row, -1).reshape(-1), G_DEV)
    pre_out = mm(grid_latent, out_grid) + mm(dec_hot, low(mm(arrived, out_mesh)))
    hid_out, slope_out = silu_both(pre_out)
    delta = low(mm(out_second, hid_out, 1, 1))

    g_out = low(wide(low(mm(grid_cot, out_second, 0, 0))) * slope_out)
    g_out_mesh = low(mm(dec_hot, g_out, 0, 0))
    g_sent = route(low(mm(g_out_mesh, out_mesh, 1, 1)))
    g_final = low(mm(pick_hot, g_sent, 0, 0))
    g_node = low(wide(low(mm(g_final, node_out, 1, 1))) * slope_node)
    g_joined = mm(g_node, node_in, 1, 1)
    g_own = wide(g_final) + g_joined[:, :width]
    g_sum = low(g_joined[:, width:])
    g_hid = low(mm(g_sum, edge_out, 1, 1))
    g_edge = low(mm(own_hot, g_hid) * slope_edge)
    g_mapped = low(mm(edge_hot, g_edge, 0, 0))
    g_send_map, g_own_map = g_mapped[:span], g_mapped[span:]
    g_extended = mm(g_send_map, edge_in_send, 1, 1)

    to_down, to_up = exchange(
        low(g_extended[halo + part :]), low(g_extended[:halo])
    )
    early_whole = join_grads(
        (
            jnp.concatenate(
                [mm(g_send_map, extended, 0, 0), mm(g_own_map, latent, 0, 0)], axis=1
            ),
            mm(g_sum, hid_sum, 0, 0),
            mm(g_node, joined, 0, 0),
            mm(g_final, hid_node, 0, 0),
            jnp.concatenate(
                [mm(g_out, grid_latent, 0, 0), mm(g_out_mesh, arrived, 0, 0)], axis=1
            ),
            mm(hid_out, grid_cot, 0, 1),
        )
    )

    to_down, to_up, early_whole = lax.optimization_barrier((to_down, to_up, early_whole))
    early_part = lax.psum_scatter(early_whole, "grid", scatter_dimension=0, tiled=True)
    g_table = (
        g_extended[halo : halo + part]
        + mm(down_hot, to_down, 0, 0)
        + mm(up_hot, to_up, 0, 0)
    )
    shares = lax.all_to_all(low(g_table), "grid", split_axis=0, concat_axis=0, tiled=True)
    g_latent = (
        g_own
        + mm(g_own_map, edge_in_own, 1, 1)
        + jnp.sum(wide(shares).reshape(n_grid, MESH_DEV, width), axis=0)
    )
    g_latent = wide(low(g_latent))
    normal = total * scale
    g_total = low(
        scale * (g_latent - normal * jnp.mean(g_latent * normal, axis=-1, keepdims=True))
    )
    g_msg = route(low(mm(enc_hot, g_total, 0, 0)))

    g_pre = low(wide(g_msg) * slope_msg)
    g_rows = low(mm(g_pre, edge_weight, 1, 1))
    g_grid = low(mm(g_out, out_grid, 1, 1) + mm(send_hot, g_rows, 0, 0))
    g_embed = low(wide(low(mm(g_grid, embed_second, 1, 1))) * slope_embed)
    late_whole = join_grads(
        (
            mm(g_embed, grid_in, 0, 1),
            mm(g_grid, hid_embed, 0, 0),
            mm(g_pre, rows, 0, 0),
            mm(g_pre, enc_feat, 0, 1),
        )
    )
    channels = grid_in.shape[0]
    late_whole, early_part = lax.optimization_barrier((late_whole, early_part))
    early_part = lax.psum_scatter(early_part, "mesh", scatter_dimension=0, tiled=True)
    late = split_grads(
        halving_scatter(late_whole), (channels, width, width, enc_feat.shape[0])
    )
    early = split_grads(
        early_part, (2 * width, width, 2 * width, width, 2 * width, channels)
    )
    layer = [grad[None] for grad in early[:4]]
    return (delta,) + tuple(late) + tuple(layer) + tuple(early[4:])


def solution(mesh):
    return jax.shard_map(
        on_device,
        mesh=mesh,
        in_specs=(
            P(None, ("groups", "grid", "mesh")),
            P(None, ("groups", "grid", "mesh")),
            P(("grid", "mesh"), None),
            P(None, ("grid", "mesh")),
            P(("grid", "mesh"), None),
            P(("grid", "mesh")),
            P("mesh"),
            P("mesh"),
            P(("grid", "mesh")),
            P(("grid", "mesh")),
            P(("grid", "mesh"), None),
            P(("grid", "mesh"), None),
            P(("grid", "mesh")),
            P(),
            P(),
            P(),
            P(),
            P(),
            P(),
            P(),
            P(),
            P(),
            P(),
        ),
        out_specs=(
            P(None, ("groups", "grid", "mesh")),
            P("groups", ("grid", "mesh")),
            P("groups", ("grid", "mesh")),
            P("groups", ("grid", "mesh")),
            P("groups", ("grid", "mesh")),
            P("groups", None, ("grid", "mesh")),
            P("groups", None, ("grid", "mesh")),
            P("groups", None, ("grid", "mesh")),
            P("groups", None, ("grid", "mesh")),
            P("groups", ("grid", "mesh")),
            P("groups", ("grid", "mesh")),
        ),
        check_vma=False,
    )
```

```python
import functools

import jax
import jax.numpy as jnp
from jax import lax
from jax.experimental import pallas as pl
from jax.experimental.pallas import tpu as pltpu
from jax.sharding import PartitionSpec as P

G_DEV = 512
MESH_DEV = 64
LOW = jnp.bfloat16
TILE = ("grid", "mesh")


def mm(left, right, over_left=1, over_right=0):
    return lax.dot_general(
        left,
        right,
        (((over_left,), (over_right,)), ((), ())),
        preferred_element_type=jnp.float32,
    )


def low(values):
    return values.astype(LOW)


def wide(values):
    return values.astype(jnp.float32)


def hot(targets, count):
    return low(targets[:, None] == lax.broadcasted_iota(jnp.int32, (1, count), 1))


def hot_columns(targets, count):
    return low(targets[None, :] == lax.broadcasted_iota(jnp.int32, (count, 1), 0))


def silu_both(value):
    gate = 1.0 / (1.0 + jnp.exp(-value))
    return low(value * gate), gate * (1.0 + value * (1.0 - gate))


def route(values):
    return lax.all_to_all(values, TILE, split_axis=0, concat_axis=0, tiled=True)


def exchange(to_next, to_previous):
    count = lax.axis_size("mesh")
    forward = [(i, i + 1) for i in range(count - 1)]
    backward = [(i + 1, i) for i in range(count - 1)]
    from_previous = lax.ppermute(to_next, "mesh", forward)
    from_next = lax.ppermute(to_previous, "mesh", backward)
    return from_previous, from_next


def products_kernel(count, out_ref_at, *refs):
    out_ref = refs[2 * count]
    for index, start in enumerate(out_ref_at):
        left, right = refs[2 * index], refs[2 * index + 1]
        size = right.shape[1]
        out_ref[:, start : start + size] = lax.dot_general(
            left[...], right[...], (((0,), (0,)), ((), ())), preferred_element_type=jnp.float32
        ).astype(LOW)


def products(pairs):
    starts = []
    operands = []
    columns = 0
    for left, right in pairs:
        starts.append(columns)
        columns += right.shape[1]
        operands += [left, right]
    return pl.pallas_call(
        functools.partial(products_kernel, len(pairs), tuple(starts)),
        out_shape=jax.ShapeDtypeStruct((operands[0].shape[1], columns), LOW),
        in_specs=[pl.BlockSpec(memory_space=pltpu.VMEM)] * len(operands),
        out_specs=pl.BlockSpec(memory_space=pltpu.VMEM),
        compiler_params=pltpu.CompilerParams(vmem_limit_bytes=32 * 2**20),
        cost_estimate=pl.CostEstimate(
            flops=0, bytes_accessed=6000 * columns, transcendentals=0
        ),
    )(*operands)


def turned(values):
    extra = -values.shape[0] % 128
    return jnp.pad(values, ((0, extra), (0, 0))).T


def split_grads(part, sizes):
    part = wide(part)
    outs = []
    start = 0
    for size in sizes:
        outs.append(part[:, start : start + size].T)
        start += size + (-size % 128)
    return outs


def plan_of(counts, order):
    left = dict(counts)
    bit = {"grid": 1, "mesh": 1}
    plan = []
    for axis in order:
        plan.append((axis, bit[axis], left["grid"], left["mesh"]))
        left[axis] //= 2
        bit[axis] *= 2
    return plan


def pieces_of(step, mine, rows):
    axis, bit, grids, meshes = step
    own = (mine[axis] // bit) % 2
    other = 1 - own
    pieces = []
    if axis == "grid":
        size = meshes * rows
        for high in range(grids // 2):
            pieces.append(((2 * high + own) * size, (2 * high + other) * size, high * size, size))
    else:
        for block in range(grids):
            for high in range(meshes // 2):
                base = block * meshes + 2 * high
                target = (block * (meshes // 2) + high) * rows
                pieces.append(((base + own) * rows, (base + other) * rows, target, rows))
    return pieces


def halving_kernel(counts, rows, spans, plans, x_ref, out_ref, *scratch):
    depth = len(plans[0])
    sums = [scratch[c * depth : (c + 1) * depth - 1] for c in range(len(spans))]
    base = len(spans) * depth
    lands = [scratch[base + c * depth : base + (c + 1) * depth] for c in range(len(spans))]
    sends, arrivals = scratch[-2], scratch[-1]
    mine = {"grid": lax.axis_index("grid"), "mesh": lax.axis_index("mesh")}

    def partner(axis, bit):
        return mine[axis] + bit * (1 - 2 * ((mine[axis] // bit) % 2))

    partners = {(axis, bit) for axis, bit, _, _ in plans[0]}
    barrier = pltpu.get_barrier_semaphore()
    for axis, bit in sorted(partners):
        pl.semaphore_signal(
            barrier,
            inc=1,
            device_id={axis: partner(axis, bit)},
            device_id_type=pl.DeviceIdType.MESH,
        )
    pl.semaphore_wait(barrier, len(partners))

    started = []
    number = 0
    flying = {}

    def source(c, s):
        return (x_ref, spans[c][0]) if s == 0 else (sums[c][s - 1], 0)

    def start(c, s):
        nonlocal number
        axis, bit, _, _ = plans[c][s]
        ref, first = source(c, s)
        copies = []
        for _, away, target, size in pieces_of(plans[c][s], mine, rows):
            copy = pltpu.make_async_remote_copy(
                src_ref=ref.at[pl.ds(pl.multiple_of(away, 16), size), pl.ds(first, spans[c][1])],
                dst_ref=lands[c][s].at[pl.ds(target, size), :],
                send_sem=sends.at[number],
                recv_sem=arrivals.at[number],
                device_id={axis: partner(axis, bit)},
                device_id_type=pl.DeviceIdType.MESH,
            )
            number += 1
            copy.start()
            copies.append(copy)
            started.append(copy)
        flying[c, s] = copies

    def finish(c, s):
        ref, first = source(c, s)
        pieces = pieces_of(plans[c][s], mine, rows)
        for copy, (keep, _, target, size) in zip(flying[c, s], pieces):
            copy.wait_recv()
            value = ref[pl.ds(pl.multiple_of(keep, 16), size), pl.ds(first, spans[c][1])].astype(
                jnp.float32
            ) + lands[c][s][pl.ds(target, size), :].astype(jnp.float32)
            if s == depth - 1:
                out_ref[:, pl.ds(spans[c][0], spans[c][1])] = value
            else:
                sums[c][s][pl.ds(target, size), :] = value.astype(LOW)

    for c in range(len(spans)):
        start(c, 0)
    for s in range(depth):
        for c in range(len(spans)):
            finish(c, s)
            if s + 1 < depth:
                start(c, s + 1)
    for copy in started:
        copy.wait_send()


def halving_scatter(whole):
    counts = {"grid": lax.axis_size("grid"), "mesh": lax.axis_size("mesh")}
    tiles = counts["grid"] * counts["mesh"]
    rows = whole.shape[0] // tiles
    if rows % 16 or counts["grid"] & (counts["grid"] - 1) or counts["mesh"] & (counts["mesh"] - 1):
        return lax.psum_scatter(whole, TILE, scatter_dimension=0, tiled=True)
    columns = whole.shape[1]
    grid_steps = ["grid"] * (counts["grid"].bit_length() - 1)
    mesh_steps = ["mesh"] * (counts["mesh"].bit_length() - 1)
    cut = (columns * 6 // 10) // 128 * 128
    spans = ((0, cut), (cut, columns - cut))
    orders = (grid_steps + mesh_steps, grid_steps[:1] + mesh_steps + grid_steps[1:])
    plans = [plan_of(counts, order) for order in orders]
    depth = len(plans[0])
    heights = [whole.shape[0] >> (s + 1) for s in range(depth)]
    sums = []
    lands = []
    for _, size in spans:
        sums += [pltpu.VMEM((heights[s], size), LOW) for s in range(depth)]
        lands += [pltpu.VMEM((heights[s], size), LOW) for s in range(depth)]
    fake = {"grid": 0, "mesh": 0}
    total = sum(len(pieces_of(step, fake, rows)) for plan in plans for step in plan)
    return pl.pallas_call(
        functools.partial(halving_kernel, counts, rows, spans, plans),
        out_shape=jax.ShapeDtypeStruct((rows, columns), jnp.float32),
        in_specs=[pl.BlockSpec(memory_space=pltpu.VMEM)],
        out_specs=pl.BlockSpec(memory_space=pltpu.VMEM),
        scratch_shapes=sums
        + lands
        + [pltpu.SemaphoreType.DMA((total,)), pltpu.SemaphoreType.DMA((total,))],
        compiler_params=pltpu.CompilerParams(
            collective_id=1, has_side_effects=True, vmem_limit_bytes=24 * 2**20
        ),
        cost_estimate=pl.CostEstimate(flops=0, bytes_accessed=90 * 10**6, transcendentals=0),
    )(whole)


def on_device(
    grid_in,
    grid_cot,
    enc_src,
    enc_feat,
    enc_dst,
    enc_count,
    halo_up,
    halo_down,
    proc_src,
    proc_dst,
    dec_send,
    dec_row,
    dec_count,
    embed_first,
    embed_second,
    edge_weight,
    feature_weight,
    layer_edge_in,
    layer_edge_out,
    layer_node_in,
    layer_node_out,
    out_first,
    out_second,
):
    width = embed_second.shape[0]
    halo = halo_up.shape[0]
    capacity = enc_src.shape[1]
    dec_capacity = dec_send.shape[1]
    n_grid = lax.axis_size("grid")
    part = MESH_DEV * n_grid
    span = part + 2 * halo
    edge_in, edge_out = layer_edge_in[0], layer_edge_out[0]
    node_in, node_out = layer_node_in[0], layer_node_out[0]
    edge_in_send, edge_in_own = edge_in[:width], edge_in[width:]
    out_grid, out_mesh = out_first[:width], out_first[width:]

    pre_embed = mm(grid_in, embed_first, 0, 0)
    hid_embed, slope_embed = silu_both(pre_embed)
    grid_latent = low(mm(hid_embed, embed_second))

    send_hot = hot(enc_src.reshape(-1), G_DEV)
    rows = low(mm(send_hot, grid_latent))
    msg, slope_msg = silu_both(mm(rows, edge_weight) + mm(enc_feat, feature_weight, 0, 0))
    received = route(msg)

    enc_valid = jnp.arange(capacity, dtype=jnp.int32)[None, :] < enc_count[:, None]
    enc_hot = hot_columns(jnp.where(enc_valid, enc_dst, -1).reshape(-1), MESH_DEV)
    total = mm(enc_hot, received)
    scale = lax.rsqrt(jnp.mean(total * total, axis=-1, keepdims=True) + 1e-05)
    latent = low(total * scale)

    table = lax.all_gather(latent, "grid", axis=0, tiled=True)
    up_hot, down_hot = hot(halo_up, part), hot(halo_down, part)
    below, above = exchange(low(mm(up_hot, table)), low(mm(down_hot, table)))
    extended = jnp.concatenate([below, table, above], axis=0)

    mapped = low(
        jnp.concatenate([mm(extended, edge_in_send), mm(latent, edge_in_own)], axis=0)
    )
    places = lax.broadcasted_iota(jnp.int32, (1, span + MESH_DEV), 1)
    edge_hot = low(
        (proc_src[:, None] == places) | ((proc_dst + span)[:, None] == places)
    )
    own_hot = hot(proc_dst, MESH_DEV)
    hid_edge, slope_edge = silu_both(mm(edge_hot, mapped))
    hid_sum = low(mm(own_hot, hid_edge, 0, 0))
    edge_sum = low(mm(hid_sum, edge_out))
    joined = jnp.concatenate([latent, edge_sum], axis=1)
    hid_node, slope_node = silu_both(mm(joined, node_in))
    final = low(wide(latent) + mm(hid_node, node_out))

    pick_hot = hot(dec_send.reshape(-1), MESH_DEV)
    arrived = route(low(mm(pick_hot, final)))

    dec_valid = jnp.arange(dec_capacity, dtype=jnp.int32)[None, :] < dec_count[:, None]
    dec_hot = hot_columns(jnp.where(dec_valid, dec_row, -1).reshape(-1), G_DEV)
    pre_out = mm(grid_latent, out_grid) + mm(dec_hot, low(mm(arrived, out_mesh)))
    hid_out, slope_out = silu_both(pre_out)
    delta = low(mm(out_second, hid_out, 1, 1))

    g_out = low(wide(low(mm(grid_cot, out_second, 0, 0))) * slope_out)
    g_out_mesh = low(mm(dec_hot, g_out, 0, 0))
    g_sent = route(low(mm(g_out_mesh, out_mesh, 1, 1)))
    g_final = low(mm(pick_hot, g_sent, 0, 0))
    g_node = low(wide(low(mm(g_final, node_out, 1, 1))) * slope_node)
    g_joined = mm(g_node, node_in, 1, 1)
    g_own = wide(g_final) + g_joined[:, :width]
    g_sum = low(g_joined[:, width:])
    g_hid = low(mm(g_sum, edge_out, 1, 1))
    g_edge = low(mm(own_hot, g_hid) * slope_edge)
    g_mapped = low(mm(edge_hot, g_edge, 0, 0))
    g_send_map, g_own_map = g_mapped[:span], g_mapped[span:]
    g_extended = mm(g_send_map, edge_in_send, 1, 1)

    to_down, to_up = exchange(
        low(g_extended[halo + part :]), low(g_extended[:halo])
    )
    early_whole = products(
        (
            (g_send_map, extended),
            (g_own_map, latent),
            (g_sum, hid_sum),
            (g_node, joined),
            (g_final, hid_node),
            (g_out, grid_latent),
            (g_out_mesh, arrived),
            (hid_out, turned(grid_cot)),
        )
    )
    to_down, to_up, early_whole = lax.optimization_barrier((to_down, to_up, early_whole))
    early_part = lax.psum_scatter(early_whole, "grid", scatter_dimension=0, tiled=True)
    g_table = (
        g_extended[halo : halo + part]
        + mm(down_hot, to_down, 0, 0)
        + mm(up_hot, to_up, 0, 0)
    )
    shares = lax.all_to_all(low(g_table), "grid", split_axis=0, concat_axis=0, tiled=True)
    g_latent = (
        g_own
        + mm(g_own_map, edge_in_own, 1, 1)
        + jnp.sum(wide(shares).reshape(n_grid, MESH_DEV, width), axis=0)
    )
    g_latent = wide(low(g_latent))
    normal = total * scale
    g_total = low(
        scale * (g_latent - normal * jnp.mean(g_latent * normal, axis=-1, keepdims=True))
    )
    g_msg = route(low(mm(enc_hot, g_total, 0, 0)))

    g_pre = low(wide(g_msg) * slope_msg)
    g_rows = low(mm(g_pre, edge_weight, 1, 1))
    g_grid = low(mm(g_out, out_grid, 1, 1) + mm(send_hot, g_rows, 0, 0))
    g_embed = low(wide(low(mm(g_grid, embed_second, 1, 1))) * slope_embed)
    late_whole = products(
        (
            (g_embed, turned(grid_in)),
            (g_grid, hid_embed),
            (g_pre, rows),
            (g_pre, turned(enc_feat)),
        )
    )
    channels = grid_in.shape[0]
    late_whole, early_part = lax.optimization_barrier((late_whole, early_part))
    early_part = lax.psum_scatter(early_part, "mesh", scatter_dimension=0, tiled=True)
    late = split_grads(
        halving_scatter(late_whole), (channels, width, width, enc_feat.shape[0])
    )
    early = split_grads(
        early_part, (2 * width, width, 2 * width, width, 2 * width, channels)
    )
    layer = [grad[None] for grad in early[:4]]
    return (delta,) + tuple(late) + tuple(layer) + tuple(early[4:])


def solution(mesh):
    return jax.shard_map(
        on_device,
        mesh=mesh,
        in_specs=(
            P(None, ("groups", "grid", "mesh")),
            P(None, ("groups", "grid", "mesh")),
            P(("grid", "mesh"), None),
            P(None, ("grid", "mesh")),
            P(("grid", "mesh"), None),
            P(("grid", "mesh")),
            P("mesh"),
            P("mesh"),
            P(("grid", "mesh")),
            P(("grid", "mesh")),
            P(("grid", "mesh"), None),
            P(("grid", "mesh"), None),
            P(("grid", "mesh")),
            P(),
            P(),
            P(),
            P(),
            P(),
            P(),
            P(),
            P(),
            P(),
            P(),
        ),
        out_specs=(
            P(None, ("groups", "grid", "mesh")),
            P("groups", ("grid", "mesh")),
            P("groups", ("grid", "mesh")),
            P("groups", ("grid", "mesh")),
            P("groups", ("grid", "mesh")),
            P("groups", None, ("grid", "mesh")),
            P("groups", None, ("grid", "mesh")),
            P("groups", None, ("grid", "mesh")),
            P("groups", None, ("grid", "mesh")),
            P("groups", ("grid", "mesh")),
            P("groups", ("grid", "mesh")),
        ),
        check_vma=False,
    )
```

```python
import functools

import jax
import jax.numpy as jnp
from jax import lax
from jax.experimental import pallas as pl
from jax.experimental.pallas import tpu as pltpu
from jax.sharding import PartitionSpec as P

G_DEV = 512
MESH_DEV = 64
LOW = jnp.bfloat16
TILE = ("grid", "mesh")


def mm(left, right, over_left=1, over_right=0):
    return lax.dot_general(
        left,
        right,
        (((over_left,), (over_right,)), ((), ())),
        preferred_element_type=jnp.float32,
    )


def low(values):
    return values.astype(LOW)


def wide(values):
    return values.astype(jnp.float32)


def hot(targets, count):
    return low(targets[:, None] == lax.broadcasted_iota(jnp.int32, (1, count), 1))


def hot_columns(targets, count):
    return low(targets[None, :] == lax.broadcasted_iota(jnp.int32, (count, 1), 0))


def silu_both(value):
    gate = 1.0 / (1.0 + jnp.exp(-value))
    return low(value * gate), gate * (1.0 + value * (1.0 - gate))


def route(values):
    return lax.all_to_all(values, TILE, split_axis=0, concat_axis=0, tiled=True)


def exchange(to_next, to_previous):
    count = lax.axis_size("mesh")
    forward = [(i, i + 1) for i in range(count - 1)]
    backward = [(i + 1, i) for i in range(count - 1)]
    from_previous = lax.ppermute(to_next, "mesh", forward)
    from_next = lax.ppermute(to_previous, "mesh", backward)
    return from_previous, from_next


def products_kernel(count, out_ref_at, *refs):
    out_ref = refs[2 * count]
    for index, start in enumerate(out_ref_at):
        left, right = refs[2 * index], refs[2 * index + 1]
        size = right.shape[1]
        out_ref[:, start : start + size] = lax.dot_general(
            left[...], right[...], (((0,), (0,)), ((), ())), preferred_element_type=jnp.float32
        ).astype(LOW)


def products(pairs):
    starts = []
    operands = []
    columns = 0
    for left, right in pairs:
        starts.append(columns)
        columns += right.shape[1]
        operands += [left, right]
    return pl.pallas_call(
        functools.partial(products_kernel, len(pairs), tuple(starts)),
        out_shape=jax.ShapeDtypeStruct((operands[0].shape[1], columns), LOW),
        in_specs=[pl.BlockSpec(memory_space=pltpu.VMEM)] * len(operands),
        out_specs=pl.BlockSpec(memory_space=pltpu.VMEM),
        compiler_params=pltpu.CompilerParams(vmem_limit_bytes=32 * 2**20),
        cost_estimate=pl.CostEstimate(
            flops=0, bytes_accessed=6000 * columns, transcendentals=0
        ),
    )(*operands)


def turned(values):
    extra = -values.shape[0] % 128
    return jnp.pad(values, ((0, extra), (0, 0))).T


def split_grads(part, sizes):
    part = wide(part)
    outs = []
    start = 0
    for size in sizes:
        outs.append(part[:, start : start + size].T)
        start += size + (-size % 128)
    return outs


def plan_of(counts, order):
    left = dict(counts)
    bit = {"grid": 1, "mesh": 1}
    plan = []
    for axis in order:
        plan.append((axis, bit[axis], left["grid"], left["mesh"]))
        left[axis] //= 2
        bit[axis] *= 2
    return plan


def pieces_of(step, mine, rows):
    axis, bit, grids, meshes = step
    own = (mine[axis] // bit) % 2
    other = 1 - own
    pieces = []
    if axis == "grid":
        size = meshes * rows
        for high in range(grids // 2):
            pieces.append(((2 * high + own) * size, (2 * high + other) * size, high * size, size))
    else:
        for block in range(grids):
            for high in range(meshes // 2):
                base = block * meshes + 2 * high
                target = (block * (meshes // 2) + high) * rows
                pieces.append(((base + own) * rows, (base + other) * rows, target, rows))
    return pieces


def halving_kernel(counts, rows, spans, plans, x_ref, out_ref, *scratch):
    depth = len(plans[0])
    sums = [scratch[c * depth : (c + 1) * depth - 1] for c in range(len(spans))]
    base = len(spans) * depth
    lands = [scratch[base + c * depth : base + (c + 1) * depth] for c in range(len(spans))]
    sends, arrivals = scratch[-2], scratch[-1]
    mine = {"grid": lax.axis_index("grid"), "mesh": lax.axis_index("mesh")}

    def partner(axis, bit):
        return mine[axis] + bit * (1 - 2 * ((mine[axis] // bit) % 2))

    partners = {(axis, bit) for axis, bit, _, _ in plans[0]}
    barrier = pltpu.get_barrier_semaphore()
    for axis, bit in sorted(partners):
        pl.semaphore_signal(
            barrier,
            inc=1,
            device_id={axis: partner(axis, bit)},
            device_id_type=pl.DeviceIdType.MESH,
        )
    pl.semaphore_wait(barrier, len(partners))

    started = []
    number = 0
    flying = {}

    def source(c, s):
        return (x_ref, spans[c][0]) if s == 0 else (sums[c][s - 1], 0)

    def start(c, s):
        nonlocal number
        axis, bit, _, _ = plans[c][s]
        ref, first = source(c, s)
        copies = []
        for _, away, target, size in pieces_of(plans[c][s], mine, rows):
            copy = pltpu.make_async_remote_copy(
                src_ref=ref.at[pl.ds(pl.multiple_of(away, 16), size), pl.ds(first, spans[c][1])],
                dst_ref=lands[c][s].at[pl.ds(target, size), :],
                send_sem=sends.at[number],
                recv_sem=arrivals.at[number],
                device_id={axis: partner(axis, bit)},
                device_id_type=pl.DeviceIdType.MESH,
            )
            number += 1
            copy.start()
            copies.append(copy)
            started.append(copy)
        flying[c, s] = copies

    def finish(c, s):
        ref, first = source(c, s)
        pieces = pieces_of(plans[c][s], mine, rows)
        for copy, (keep, _, target, size) in zip(flying[c, s], pieces):
            copy.wait_recv()
            value = ref[pl.ds(pl.multiple_of(keep, 16), size), pl.ds(first, spans[c][1])].astype(
                jnp.float32
            ) + lands[c][s][pl.ds(target, size), :].astype(jnp.float32)
            if s == depth - 1:
                out_ref[:, pl.ds(spans[c][0], spans[c][1])] = value
            else:
                sums[c][s][pl.ds(target, size), :] = value.astype(LOW)

    for c in range(len(spans)):
        start(c, 0)
    for s in range(depth):
        for c in range(len(spans)):
            finish(c, s)
            if s + 1 < depth:
                start(c, s + 1)
    for copy in started:
        copy.wait_send()


def halving_scatter(whole):
    counts = {"grid": lax.axis_size("grid"), "mesh": lax.axis_size("mesh")}
    tiles = counts["grid"] * counts["mesh"]
    rows = whole.shape[0] // tiles
    if rows % 16 or counts["grid"] & (counts["grid"] - 1) or counts["mesh"] & (counts["mesh"] - 1):
        return lax.psum_scatter(whole, TILE, scatter_dimension=0, tiled=True)
    columns = whole.shape[1]
    grid_steps = ["grid"] * (counts["grid"].bit_length() - 1)
    mesh_steps = ["mesh"] * (counts["mesh"].bit_length() - 1)
    cut = (columns * 6 // 10) // 128 * 128
    spans = ((0, cut), (cut, columns - cut))
    orders = (grid_steps + mesh_steps, grid_steps[:1] + mesh_steps + grid_steps[1:])
    plans = [plan_of(counts, order) for order in orders]
    depth = len(plans[0])
    heights = [whole.shape[0] >> (s + 1) for s in range(depth)]
    sums = []
    lands = []
    for _, size in spans:
        sums += [pltpu.VMEM((heights[s], size), LOW) for s in range(depth)]
        lands += [pltpu.VMEM((heights[s], size), LOW) for s in range(depth)]
    fake = {"grid": 0, "mesh": 0}
    total = sum(len(pieces_of(step, fake, rows)) for plan in plans for step in plan)
    return pl.pallas_call(
        functools.partial(halving_kernel, counts, rows, spans, plans),
        out_shape=jax.ShapeDtypeStruct((rows, columns), jnp.float32),
        in_specs=[pl.BlockSpec(memory_space=pltpu.VMEM)],
        out_specs=pl.BlockSpec(memory_space=pltpu.VMEM),
        scratch_shapes=sums
        + lands
        + [pltpu.SemaphoreType.DMA((total,)), pltpu.SemaphoreType.DMA((total,))],
        compiler_params=pltpu.CompilerParams(
            collective_id=1, has_side_effects=True, vmem_limit_bytes=24 * 2**20
        ),
        cost_estimate=pl.CostEstimate(flops=0, bytes_accessed=90 * 10**6, transcendentals=0),
    )(whole)


def on_device(
    grid_in,
    grid_cot,
    enc_src,
    enc_feat,
    enc_dst,
    enc_count,
    halo_up,
    halo_down,
    proc_src,
    proc_dst,
    dec_send,
    dec_row,
    dec_count,
    embed_first,
    embed_second,
    edge_weight,
    feature_weight,
    layer_edge_in,
    layer_edge_out,
    layer_node_in,
    layer_node_out,
    out_first,
    out_second,
):
    width = embed_second.shape[0]
    halo = halo_up.shape[0]
    capacity = enc_src.shape[1]
    dec_capacity = dec_send.shape[1]
    n_grid = lax.axis_size("grid")
    part = MESH_DEV * n_grid
    span = part + 2 * halo
    edge_in, edge_out = layer_edge_in[0], layer_edge_out[0]
    node_in, node_out = layer_node_in[0], layer_node_out[0]
    edge_in_send, edge_in_own = edge_in[:width], edge_in[width:]
    out_grid, out_mesh = out_first[:width], out_first[width:]

    pre_embed = mm(grid_in, embed_first, 0, 0)
    hid_embed, slope_embed = silu_both(pre_embed)
    grid_latent = low(mm(hid_embed, embed_second))

    send_hot = hot(enc_src.reshape(-1), G_DEV)
    rows = low(mm(send_hot, grid_latent))
    msg, slope_msg = silu_both(mm(rows, edge_weight) + mm(enc_feat, feature_weight, 0, 0))
    received = route(msg)

    enc_valid = jnp.arange(capacity, dtype=jnp.int32)[None, :] < enc_count[:, None]
    enc_hot = hot_columns(jnp.where(enc_valid, enc_dst, -1).reshape(-1), MESH_DEV)
    total = mm(enc_hot, received)
    scale = lax.rsqrt(jnp.mean(total * total, axis=-1, keepdims=True) + 1e-05)
    latent = low(total * scale)

    table = lax.all_gather(latent, "grid", axis=0, tiled=True)
    up_hot, down_hot = hot(halo_up, part), hot(halo_down, part)
    below, above = exchange(low(mm(up_hot, table)), low(mm(down_hot, table)))
    extended = jnp.concatenate([below, table, above], axis=0)

    mapped = low(
        jnp.concatenate([mm(extended, edge_in_send), mm(latent, edge_in_own)], axis=0)
    )
    places = lax.broadcasted_iota(jnp.int32, (1, span + MESH_DEV), 1)
    edge_hot = low(
        (proc_src[:, None] == places) | ((proc_dst + span)[:, None] == places)
    )
    own_hot = hot(proc_dst, MESH_DEV)
    hid_edge, slope_edge = silu_both(mm(edge_hot, mapped))
    hid_sum = low(mm(own_hot, hid_edge, 0, 0))
    edge_sum = low(mm(hid_sum, edge_out))
    joined = jnp.concatenate([latent, edge_sum], axis=1)
    hid_node, slope_node = silu_both(mm(joined, node_in))
    final = low(wide(latent) + mm(hid_node, node_out))

    pick_hot = hot(dec_send.reshape(-1), MESH_DEV)
    arrived = route(low(mm(pick_hot, final)))

    dec_valid = jnp.arange(dec_capacity, dtype=jnp.int32)[None, :] < dec_count[:, None]
    dec_hot = hot_columns(jnp.where(dec_valid, dec_row, -1).reshape(-1), G_DEV)
    pre_out = mm(grid_latent, out_grid) + mm(dec_hot, low(mm(arrived, out_mesh)))
    hid_out, slope_out = silu_both(pre_out)
    delta = low(mm(out_second, hid_out, 1, 1))

    g_out = low(wide(low(mm(grid_cot, out_second, 0, 0))) * slope_out)
    g_out_mesh = low(mm(dec_hot, g_out, 0, 0))
    g_sent = route(low(mm(g_out_mesh, out_mesh, 1, 1)))
    g_final = low(mm(pick_hot, g_sent, 0, 0))
    g_node = low(wide(low(mm(g_final, node_out, 1, 1))) * slope_node)
    g_joined = mm(g_node, node_in, 1, 1)
    g_own = wide(g_final) + g_joined[:, :width]
    g_sum = low(g_joined[:, width:])
    g_hid = low(mm(g_sum, edge_out, 1, 1))
    g_edge = low(mm(own_hot, g_hid) * slope_edge)
    g_mapped = low(mm(edge_hot, g_edge, 0, 0))
    g_send_map, g_own_map = g_mapped[:span], g_mapped[span:]
    g_extended = mm(g_send_map, edge_in_send, 1, 1)

    to_down, to_up = exchange(
        low(g_extended[halo + part :]), low(g_extended[:halo])
    )
    early_whole = products(
        (
            (g_send_map, extended),
            (g_own_map, latent),
            (g_sum, hid_sum),
            (g_node, joined),
            (g_final, hid_node),
            (g_out, grid_latent),
            (g_out_mesh, arrived),
        )
    )
    to_down, to_up, early_whole = lax.optimization_barrier((to_down, to_up, early_whole))
    early_part = lax.psum_scatter(early_whole, "grid", scatter_dimension=0, tiled=True)
    g_table = (
        g_extended[halo : halo + part]
        + mm(down_hot, to_down, 0, 0)
        + mm(up_hot, to_up, 0, 0)
    )
    shares = lax.all_to_all(low(g_table), "grid", split_axis=0, concat_axis=0, tiled=True)
    g_latent = (
        g_own
        + mm(g_own_map, edge_in_own, 1, 1)
        + jnp.sum(wide(shares).reshape(n_grid, MESH_DEV, width), axis=0)
    )
    g_latent = wide(low(g_latent))
    normal = total * scale
    g_total = low(
        scale * (g_latent - normal * jnp.mean(g_latent * normal, axis=-1, keepdims=True))
    )
    g_msg = route(low(mm(enc_hot, g_total, 0, 0)))

    g_pre = low(wide(g_msg) * slope_msg)
    g_rows = low(mm(g_pre, edge_weight, 1, 1))
    g_grid = low(mm(g_out, out_grid, 1, 1) + mm(send_hot, g_rows, 0, 0))
    g_embed = low(wide(low(mm(g_grid, embed_second, 1, 1))) * slope_embed)
    late_whole = products(
        (
            (g_embed, turned(grid_in)),
            (g_grid, hid_embed),
            (g_pre, rows),
            (g_pre, turned(enc_feat)),
            (hid_out, turned(grid_cot)),
        )
    )
    channels = grid_in.shape[0]
    late_whole, early_part = lax.optimization_barrier((late_whole, early_part))
    early_part = lax.psum_scatter(early_part, "mesh", scatter_dimension=0, tiled=True)
    late = split_grads(
        halving_scatter(late_whole), (channels, width, width, enc_feat.shape[0], channels)
    )
    early = split_grads(
        early_part, (2 * width, width, 2 * width, width, 2 * width)
    )
    layer = [grad[None] for grad in early[:4]]
    return (delta,) + tuple(late[:4]) + tuple(layer) + (early[4], late[4])


def solution(mesh):
    return jax.shard_map(
        on_device,
        mesh=mesh,
        in_specs=(
            P(None, ("groups", "grid", "mesh")),
            P(None, ("groups", "grid", "mesh")),
            P(("grid", "mesh"), None),
            P(None, ("grid", "mesh")),
            P(("grid", "mesh"), None),
            P(("grid", "mesh")),
            P("mesh"),
            P("mesh"),
            P(("grid", "mesh")),
            P(("grid", "mesh")),
            P(("grid", "mesh"), None),
            P(("grid", "mesh"), None),
            P(("grid", "mesh")),
            P(),
            P(),
            P(),
            P(),
            P(),
            P(),
            P(),
            P(),
            P(),
            P(),
        ),
        out_specs=(
            P(None, ("groups", "grid", "mesh")),
            P("groups", ("grid", "mesh")),
            P("groups", ("grid", "mesh")),
            P("groups", ("grid", "mesh")),
            P("groups", ("grid", "mesh")),
            P("groups", None, ("grid", "mesh")),
            P("groups", None, ("grid", "mesh")),
            P("groups", None, ("grid", "mesh")),
            P("groups", None, ("grid", "mesh")),
            P("groups", ("grid", "mesh")),
            P("groups", ("grid", "mesh")),
        ),
        check_vma=False,
    )
```
